32 devices in a mesh: groups: 2 (over y), mpo: 4 (over z), sec: 2 (over x), rep: 2 (over core).
Axes of the slice: x: 2, y: 2, z: 4, core: 2. Of those that a mesh axis runs over, the one named last changes fastest.
Arguments:
- start_vector: float32 [4, 1024, 256], P(('groups', 'sec'), 'rep'), parts along dimension 0, may hold values from -6 to 6
- block_rows: int32 [4], P(('groups', 'sec')), parts along dimension 0, may hold values from 1 to 1024, 1536 in all
- left_blocks: bfloat16 [8, 4, 1024, 1024], P('mpo', ('groups', 'sec'), 'rep'), parts along dimension 1, as said below
- right_blocks: bfloat16 [8, 4, 256, 256], P('mpo', ('groups', 'sec')), parts along dimension 1, as said below
Outputs:
- wavefunction: float32 [4, 1024, 256], P(('groups', 'sec'), 'rep'), parts along dimension 0
- energy: float32 [2], P('groups'), parts along dimension 0
- environment: float32 [8, 4, 256, 256], P('mpo', ('groups', 'sec'), 'rep'), parts along dimension 1
The draws below stay inside these ranges and needn't reach their ends.
There are 2 independent parts, one for each index of `groups`. The reference program is written for one: setup_inputs(seed, part) draws one part's arguments, and reference() takes and returns one part's arrays. A program takes and returns all parts, laid end to end along the dimension named above; each array names one. Nothing has to cross between parts.
Inputs may be any that keep to these rules, and one draw needn't show every extreme that they name: Each block left_blocks[w, s] is symmetric. Each block right_blocks[w, s] is symmetric.
All inputs are finite; a program needn't handle non-finite values. No bound on the sum of `block_rows` on one device may be relied on, other than what follows from the above.
Results may differ from the reference program's by a relative error of at most 0.017.
Values may be sent and summed in bfloat16 or wider, within the bound.
A program may use at most 64 MiB of HBM per device.

```python
import math
import jax
import jax.numpy as jnp
import numpy as np
from jax import lax

W_DEV = 2
BLK = 1024
COLS = 256
ITERS = 4
MPOW = 8
SECTORS = 2
N_MPO = 4


def mirrored(noise, factor, scale):
    paired = (noise + jnp.swapaxes(noise, 2, 3)) * (0.7071067811865476 * scale)
    return paired * factor[:, :, :, None] * factor[:, :, None, :]


def draw_left_blocks(key, part):
    key = jax.random.fold_in(key, 11)
    noise_key, scale_key = jax.random.split(key)
    shape = (MPOW, SECTORS, BLK, BLK)
    noise = jax.random.normal(noise_key, shape, jnp.float32)
    factor = jnp.exp(jax.random.uniform(scale_key, (MPOW, SECTORS, BLK), jnp.float32, -0.3, 0.3))
    return mirrored(noise, factor, (MPOW * BLK) ** (-0.5)).astype(jnp.bfloat16)


def draw_right_blocks(key, part):
    key = jax.random.fold_in(key, 23)
    noise_key, scale_key = jax.random.split(key)
    shape = (MPOW, SECTORS, COLS, COLS)
    noise = jax.random.normal(noise_key, shape, jnp.float32)
    factor = jnp.exp(jax.random.uniform(scale_key, (MPOW, SECTORS, COLS), jnp.float32, -0.3, 0.3))
    return mirrored(noise, factor, COLS ** (-0.5)).astype(jnp.bfloat16)


def steps_of(stream_key, dims, shards, least, top_value):
    level = 1.0
    for axis_at, shards_of in shards:
        heights = jax.random.uniform(jax.random.fold_in(jax.random.fold_in(stream_key, 6), axis_at), (shards_of,), jnp.float32, least / len(shards), top_value / len(shards))
        level = level * jnp.repeat(jnp.exp(heights), dims[axis_at] // shards_of).reshape((-1,) + (1,) * (len(dims) - 1 - axis_at))
    return level


def split_up(number_of, total, limit, lean):
    loads = [(1 << 20) // math.isqrt(rank ** lean) + 1 for rank in range(2, number_of + 1)]
    surplus, counts = total - limit - (number_of - 1), [1] * (number_of - 1)
    while surplus > 0:
        candidates = [i for i in range(number_of - 1) if counts[i] < limit]
        whole, left = sum([loads[i] for i in candidates]), surplus
        for i in candidates:
            extra = min(limit - counts[i], max(1, left * loads[i] // whole), surplus)
            counts[i] = counts[i] + extra
            surplus = surplus - extra
    return np.array([limit] + counts)


def uneven_parts(key, number_of, total, most, slope):
    if number_of == 2:
        one = jax.random.randint(key, (), max(1, total - most), min(most, total - 1) + 1)
        return jnp.stack([one, total - one])
    sizes = jnp.asarray(split_up(number_of, total, most, slope), jnp.int32)
    couples = (number_of - 1) // 2
    source_of, taker = sizes[1:1 + 2 * couples:2], sizes[2:2 + 2 * couples:2]
    slack = jnp.minimum(source_of - 1, most - taker)
    passed = jax.random.randint(jax.random.fold_in(key, 1), (couples,), 0, 1 << 20) % (slack + 1)
    sizes = sizes.at[1:1 + 2 * couples:2].set(source_of - passed).at[2:2 + 2 * couples:2].set(taker + passed)
    return sizes[jax.random.permutation(jax.random.fold_in(key, 2), number_of)]


def gaussian(key, shape, deviation, limit, shards=(), kind=jnp.bfloat16):
    factor_of = steps_of(key, shape, shards, -0.22, 0.18) if shards else 1.0
    array = jax.random.normal(key, shape, jnp.float32) * deviation * factor_of
    return jnp.minimum(jnp.maximum(array, -limit), limit).astype(kind)


def setup_inputs(seed: int = 0, part: int = 0) -> dict:
    splits = jax.random.split(jax.random.key(seed), 5)
    own_keys = jax.random.split(jax.random.fold_in(splits[4], part), 5)
    start_vector = gaussian(own_keys[0], (SECTORS, BLK, COLS), 1.0, 6.0, ((0, 2), (1, 2)), jnp.float32)
    block_rows = uneven_parts(own_keys[1], SECTORS, SECTORS * BLK // 2 + BLK // 2, BLK, 0).astype(jnp.int32)
    left_blocks = draw_left_blocks(jax.random.fold_in(jax.random.fold_in(splits[4], part), 71), part)
    right_blocks = draw_right_blocks(jax.random.fold_in(jax.random.fold_in(splits[4], part), 71), part)
    return dict(start_vector=start_vector, block_rows=block_rows, left_blocks=left_blocks, right_blocks=right_blocks)


EPSILON = 1e-06

def to_narrow(values):
    rounded = lax.optimization_barrier(values.astype(jnp.bfloat16))
    return rounded.astype(jnp.float32)

def apply_operator(left_blocks, right_blocks, vector, live_rows):
    narrow = to_narrow(vector)
    left_groups = jnp.reshape(left_blocks, (N_MPO, W_DEV) + left_blocks.shape[1:])
    right_groups = jnp.reshape(right_blocks, (N_MPO, W_DEV) + right_blocks.shape[1:])

    def apply_step(summed, operands):
        left_term, right_term = operands
        partial_left = jnp.einsum('wsij,sjc->wsic', left_term.astype(jnp.float32), narrow)
        partial_left = to_narrow(partial_left)
        group_term = jnp.einsum('wsic,wscd->sid', partial_left, right_term.astype(jnp.float32))
        return (summed + to_narrow(group_term), None)
    summed, _ = lax.scan(apply_step, jnp.zeros_like(vector), (left_groups, right_groups))
    return live_rows * summed

def reference(start_vector, block_rows, left_blocks, right_blocks):
    row_ids = jnp.arange(BLK, dtype=jnp.int32)
    live_rows = (row_ids[None, :] < block_rows[:, None]).astype(jnp.float32)[:, :, None]
    masked = live_rows * start_vector
    vector = masked / jnp.sqrt(jnp.sum(masked * masked) + EPSILON)
    applied = apply_operator(left_blocks, right_blocks, vector, live_rows)
    rayleigh = jnp.sum(vector * applied)
    for iteration in range(ITERS):
        residual = applied - rayleigh * vector
        square_sum = jnp.sum(residual * residual)
        image = apply_operator(left_blocks, right_blocks, residual, live_rows)
        product_sum = jnp.sum(residual * image)
        scale = jnp.sqrt(square_sum + EPSILON)
        coupling = square_sum / scale
        curvature = product_sum / (scale * scale)
        half_gap = 0.5 * (rayleigh - curvature)
        lowest = 0.5 * (rayleigh + curvature) - jnp.sqrt(half_gap * half_gap + coupling * coupling)
        retain = lowest - curvature
        length = jnp.sqrt(retain * retain + coupling * coupling)
        vector = (retain * vector + coupling * residual / scale) / length
        applied = (retain * applied + coupling * image / scale) / length
        rayleigh = lowest
    wavefunction = vector * math.sqrt(SECTORS * BLK * COLS)
    narrow = to_narrow(wavefunction)
    env_scale = math.sqrt(MPOW / BLK)

    def env_term(left_term):
        product = to_narrow(jnp.einsum('sij,sjc->sic', left_term.astype(jnp.float32), narrow))
        return jnp.einsum('sic,sid->scd', narrow, product) * env_scale
    environment = lax.map(env_term, left_blocks)
    return (wavefunction, jnp.reshape(rayleigh, (1,)), environment)
```

```python
import functools
import math

import jax
import jax.numpy as jnp
from jax import lax
from jax.experimental import pallas as pl
from jax.experimental.pallas import tpu as pltpu
from jax.sharding import PartitionSpec as P

ITERS = 4
EPSILON = 1e-06
STEPS = ITERS + 1
CHUNKS = 8
BLOCKS = 4
LAG = 2

F32 = jnp.float32
BF16 = jnp.bfloat16
MESH = pl.DeviceIdType.MESH


def body(
    n_mpo, n_sec, block_rows, start_hbm, left_hbm, right_hbm,
    wave_ref, energy_ref, env_ref,
    start_v, left, right, u, x, prod, term, inward, sums, total, got_in, got_out,
    acc, gram, last, env_own, env_send, env_recv,
    load_sem, x_send, x_recv, in_send, in_recv, out_send, out_recv,
    gram_send, gram_recv, last_send, last_recv, env_send_sem, env_recv_sem,
):
    terms, rows, size = left.shape
    cols = right.shape[1]
    chunk = rows // CHUNKS
    block = rows // BLOCKS
    per_block = CHUNKS // BLOCKS
    n_rep = 2
    n_peer = n_sec * n_rep
    n_all = n_mpo * n_peer
    half = n_mpo // 2

    z = lax.axis_index("mpo")
    sec = lax.axis_index("sec")
    rep = lax.axis_index("rep")
    peer = sec * n_rep + rep
    every = z * n_peer + peer
    other = 1 - rep
    lower = z < half
    depth = jnp.where(lower, z, n_mpo - 1 - z)
    z_in = jnp.where(lower, z + 1, z - 1)
    z_out = jnp.where(lower, z - 1, z + 1)
    middle = depth == half - 1
    outer = depth == 0
    own_at = pl.multiple_of(rep * rows, rows)
    other_at = pl.multiple_of(other * rows, rows)

    def device_at(index):
        return {
            "mpo": index // n_peer,
            "sec": lax.rem(index, n_peer) // n_rep,
            "rep": lax.rem(index, n_rep),
        }

    start_load = pltpu.make_async_copy(start_hbm.at[0], start_v, load_sem.at[0])
    left_load = pltpu.make_async_copy(left_hbm.at[:, 0], left, load_sem.at[1])
    right_load = pltpu.make_async_copy(right_hbm.at[:, 0], right, load_sem.at[2])
    start_load.start()
    left_load.start()
    right_load.start()

    barrier = pltpu.get_barrier_semaphore()

    def greet(d, carry):
        target = lax.rem(every + d, n_all)
        pl.semaphore_signal(barrier, inc=1, device_id=device_at(target), device_id_type=MESH)
        return carry

    lax.fori_loop(1, n_all, greet, 0)

    live_count = block_rows[0] - rep * rows
    row_at = lax.broadcasted_iota(jnp.int32, (chunk, cols), 0)

    def live_of(c):
        return row_at + c * chunk < live_count

    def x_copy(k, at, count):
        return pltpu.make_async_remote_copy(
            src_ref=x.at[k, pl.ds(at, count)],
            dst_ref=x.at[k, pl.ds(at, count)],
            send_sem=x_send.at[k],
            recv_sem=x_recv.at[k],
            device_id={"rep": other},
            device_id_type=MESH,
        )

    def in_copy(k, c, to_middle):
        if to_middle:
            return pltpu.make_async_remote_copy(
                src_ref=sums.at[k, c], dst_ref=got_out.at[k, c],
                send_sem=in_send.at[k], recv_sem=out_recv.at[k, c],
                device_id={"mpo": z_in}, device_id_type=MESH,
            )
        return pltpu.make_async_remote_copy(
            src_ref=sums.at[k, c], dst_ref=got_in.at[k, c],
            send_sem=in_send.at[k], recv_sem=in_recv.at[k, c],
            device_id={"mpo": z_in}, device_id_type=MESH,
        )

    def out_copy(k, c):
        return pltpu.make_async_remote_copy(
            src_ref=total.at[k, c], dst_ref=got_out.at[k, c],
            send_sem=out_send.at[k], recv_sem=out_recv.at[k, c],
            device_id={"mpo": z_out}, device_id_type=MESH,
        )

    def gram_copy(k, d, sending):
        target = lax.rem(peer + d, n_peer)
        slot = peer if sending else lax.rem(peer - d + n_peer, n_peer)
        return pltpu.make_async_remote_copy(
            src_ref=gram.at[k, slot], dst_ref=gram.at[k, slot],
            send_sem=gram_send.at[k], recv_sem=gram_recv.at[k, d],
            device_id={"sec": target // n_rep, "rep": lax.rem(target, n_rep)},
            device_id_type=MESH,
        )

    def last_copy(d, sending):
        target = lax.rem(every + d, n_all)
        slot = every if sending else lax.rem(every - d + n_all, n_all)
        return pltpu.make_async_remote_copy(
            src_ref=last.at[slot], dst_ref=last.at[slot],
            send_sem=last_send, recv_sem=last_recv.at[d],
            device_id=device_at(target), device_id_type=MESH,
        )

    def send_inward(k, c):
        if n_mpo == 2:
            in_copy(k, c, True).start()
            return

        @pl.when(middle)
        def _():
            in_copy(k, c, True).start()

        @pl.when(jnp.logical_not(middle))
        def _():
            in_copy(k, c, False).start()

    def fold(values):
        return jnp.sum(values.reshape(chunk // 8, 8, cols), axis=0)

    def put_basis(k, c, new):
        at = pl.multiple_of(c * chunk, chunk)
        u[k, pl.ds(at, chunk)] = new
        x_at = pl.multiple_of(own_at + c * chunk, chunk)
        x[k, pl.ds(x_at, chunk)] = new.astype(BF16)
        x_copy(k, x_at, chunk).start()
        for j in range(k):
            acc[j] += fold(new * u[j, pl.ds(at, chunk)])
        acc[k] += fold(new * new)

    def whole(values):
        one = jnp.sum(jnp.sum(values, axis=0, keepdims=True), axis=1, keepdims=True)
        return jnp.broadcast_to(one, (1, cols))

    def share_gram(k):
        parts = [whole(acc[j]) for j in range(k + 1)]
        parts += [jnp.zeros((8 - k - 1, cols), F32)]
        gram[k, peer] = jnp.concatenate(parts, axis=0)
        for d in range(1, n_peer):
            gram_copy(k, d, True).start()

    def take_gram(k):
        for d in range(1, n_peer):
            gram_copy(k, d, False).wait_recv()
        summed = gram[k, 0]
        for slot in range(1, n_peer):
            summed = summed + gram[k, slot]
        return [summed[j : j + 1] for j in range(k + 1)]

    def multiply(k):
        def one(b, carry):
            at = pl.multiple_of(b * block, block)
            for w in range(terms):
                left_term = jnp.dot(
                    left[w, pl.ds(at, block)], x[k], preferred_element_type=F32
                )
                prod[k, pl.ds(at, block), w * cols : (w + 1) * cols] = left_term.astype(BF16)
            group = jnp.dot(
                prod[k, pl.ds(at, block)],
                right[...].reshape(terms * cols, cols),
                preferred_element_type=F32,
            )
            if k < ITERS:
                for i in range(per_block):
                    piece = group[i * chunk : (i + 1) * chunk]
                    c = b * per_block + i

                    @pl.when(outer)
                    def _():
                        sums[k, c] = piece.astype(BF16)
                        send_inward(k, c)

                    @pl.when(jnp.logical_not(outer))
                    def _():
                        term[c] = piece
            else:
                held = group * u[k, pl.ds(at, block)]
                acc[0] += jnp.sum(held.reshape(block // 8, 8, cols), axis=0)
            return carry

        lax.fori_loop(0, BLOCKS, one, 0)

    ups, mids, downs, grams = [], [], [], {}

    def g(i, j):
        return grams[(min(i, j), max(i, j))]

    def coefficients(k):
        here = g(k, k) + EPSILON
        inverse = lax.rsqrt(here)
        if k == 0:
            mid = jnp.zeros_like(here)
            down = jnp.zeros_like(here)
        else:
            before = g(k - 1, k - 1) + EPSILON
            lean = ups[k - 1] * g(k - 1, k)
            if k >= 2:
                lean = lean + downs[k - 1] * g(k - 2, k - 1)
            mid = mids[k - 1] + lean / before
            down = ups[k - 1] * g(k, k) / before
        ups.append(here * inverse)
        mids.append(mid)
        downs.append(down)
        return inverse

    def combine(k, inverse):
        mid, down = mids[k], downs[k]

        def finish(c):
            @pl.when(middle)
            def _():
                out_copy(k, c).wait_recv()
                sides = sums[k, c].astype(F32) + got_out[k, c].astype(F32)
                total[k, c] = sides.astype(BF16)

            @pl.when(jnp.logical_not(middle))
            def _():
                out_copy(k, c).wait_recv()
                total[k, c] = got_out[k, c]

            @pl.when(jnp.logical_not(outer))
            def _():
                out_copy(k, c).start()

            at = pl.multiple_of(c * chunk, chunk)
            applied = jnp.where(live_of(c), total[k, c].astype(F32), 0.0)
            new = applied - mid * u[k, pl.ds(at, chunk)]
            if k >= 1:
                new = new - down * u[k - 1, pl.ds(at, chunk)]
            put_basis(k + 1, c, new * inverse)

        def one(c, carry):
            @pl.when(jnp.logical_and(jnp.logical_not(outer), c < CHUNKS))
            def _():
                in_copy(k, c, False).wait_recv()
                sums[k, c] = (term[c] + got_in[k, c].astype(F32)).astype(BF16)
                send_inward(k, c)

            @pl.when(c >= LAG)
            def _():
                finish(c - LAG)

            return carry

        lax.fori_loop(0, CHUNKS + LAG, one, 0)

    def dot_of(a, b):
        result = None
        for i, left_value in a.items():
            inner = None
            for j, right_value in b.items():
                value = right_value * g(i, j)
                inner = value if inner is None else inner + value
            value = left_value * inner
            result = value if result is None else result + value
        return result

    def applied_to(a):
        result = {}

        def add(i, value):
            result[i] = value if i not in result else result[i] + value

        for k, value in a.items():
            add(k + 1, ups[k] * value)
            if k >= 1:
                add(k, mids[k] * value)
                add(k - 1, downs[k] * value)
        return result

    def mixed(first, a, second, b):
        result = {i: first * value for i, value in a.items()}
        for i, value in b.items():
            scaled = second * value
            result[i] = scaled if i not in result else result[i] + scaled
        return result

    start_load.wait()
    pl.semaphore_wait(barrier, n_all - 1)
    acc[...] = jnp.zeros_like(acc)

    def begin(c, carry):
        at = pl.multiple_of(c * chunk, chunk)
        put_basis(0, c, jnp.where(live_of(c), start_v[pl.ds(at, chunk)], 0.0))
        return carry

    lax.fori_loop(0, CHUNKS, begin, 0)
    share_gram(0)
    left_load.wait()
    right_load.wait()

    state = {}
    for k in range(STEPS):
        x_copy(k, other_at, rows).wait_recv()
        if k == ITERS:
            acc[...] = jnp.zeros_like(acc)
        multiply(k)
        if k == ITERS:
            last[every] = jnp.broadcast_to(whole(acc[0])[:, :128], (8, 128))

            def send_last(d, carry):
                last_copy(d, True).start()
                return carry

            lax.fori_loop(1, n_all, send_last, 0)
        for j, value in enumerate(take_gram(k)):
            grams[(j, k)] = value
        if k < ITERS:
            inverse = coefficients(k)
        if k == 0:
            first = lax.rsqrt(g(0, 0) + EPSILON)
            state["vector"] = {0: first}
            state["applied"] = applied_to(state["vector"])
        if k == 1:
            state["rayleigh"] = dot_of(state["vector"], state["applied"])
        if k >= 1:
            vector, applied, rayleigh = state["vector"], state["applied"], state["rayleigh"]
            if k >= 2:
                residual, square_sum = state["residual"], state["square_sum"]
                scale, coupling = state["scale"], state["coupling"]
                image = applied_to(residual)
                product_sum = dot_of(residual, image)
                curvature = product_sum / (scale * scale)
                half_gap = 0.5 * (rayleigh - curvature)
                lowest = 0.5 * (rayleigh + curvature) - jnp.sqrt(half_gap * half_gap + coupling * coupling)
                retain = lowest - curvature
                length = jnp.sqrt(retain * retain + coupling * coupling)
                one, two = retain / length, coupling / (scale * length)
                vector = mixed(one, vector, two, residual)
                applied = mixed(one, applied, two, image)
                rayleigh = lowest
            residual = mixed(1.0, applied, -rayleigh, vector)
            square_sum = dot_of(residual, residual)
            scale = jnp.sqrt(square_sum + EPSILON)
            state = dict(
                vector=vector, applied=applied, rayleigh=rayleigh, residual=residual,
                square_sum=square_sum, scale=scale, coupling=square_sum / scale,
            )
        if k < ITERS:
            acc[...] = jnp.zeros_like(acc)
            combine(k, inverse)
            share_gram(k + 1)

    vector, rayleigh, residual = state["vector"], state["rayleigh"], state["residual"]
    scale, coupling = state["scale"], state["coupling"]
    top = residual[ITERS]
    lower_part = {i: value for i, value in residual.items() if i < ITERS}
    lower_image = applied_to(lower_part)
    known = dot_of(residual, lower_image) + top * dot_of({ITERS: jnp.ones_like(top)}, lower_image)
    inverse_square = 1.0 / (scale * scale)

    def take_last(d, carry):
        last_copy(d, False).wait_recv()
        return carry

    lax.fori_loop(1, n_all, take_last, 0)
    corner = lax.fori_loop(1, n_all, lambda i, value: value + last[i, 0:1], last[0, 0:1])
    corner = jnp.broadcast_to(corner[:, 0:1], (1, cols))
    curvature = (known + top * top * corner) * inverse_square
    half_gap = 0.5 * (rayleigh - curvature)
    lowest = 0.5 * (rayleigh + curvature) - jnp.sqrt(half_gap * half_gap + coupling * coupling)
    retain = lowest - curvature
    length = jnp.sqrt(retain * retain + coupling * coupling)
    full = math.sqrt(n_sec * size * cols)
    vector = mixed(full * retain / length, vector, full * coupling / (scale * length), residual)
    energy_ref[0] = lowest[0, 0]

    def finish_rows(c, carry):
        at = pl.multiple_of(c * chunk, chunk)
        here = pl.ds(at, chunk)
        wave = vector[0] * u[0, here]
        for k in range(1, STEPS):
            wave = wave + vector[k] * u[k, here]
        wave_ref[0, here] = wave
        x[0, here] = wave.astype(BF16)
        for w in range(terms):
            span = slice(w * cols, (w + 1) * cols)
            image = vector[0] * prod[0, here, span].astype(F32)
            for k in range(1, STEPS):
                image = image + vector[k] * prod[k, here, span].astype(F32)
            prod[0, here, span] = image.astype(BF16)
        return carry

    for k in range(STEPS):
        x_copy(k, own_at, rows).wait_send()
    lax.fori_loop(0, CHUNKS, finish_rows, 0)
    env_scale = math.sqrt(terms * n_mpo / size)
    env = lax.dot_general(
        x[0, 0:rows], prod[0], (((0,), (0,)), ((), ())), preferred_element_type=F32
    ) * env_scale
    env_own[...] = env
    share = cols // n_rep
    env_send[...] = env_own[pl.ds(pl.multiple_of(other * share, share), share)].astype(BF16)
    env_copy = pltpu.make_async_remote_copy(
        src_ref=env_send, dst_ref=env_recv, send_sem=env_send_sem, recv_sem=env_recv_sem,
        device_id={"rep": other}, device_id_type=MESH,
    )
    env_copy.start()

    for k in range(ITERS):
        in_copy_all = pltpu.make_async_remote_copy(
            src_ref=sums.at[k], dst_ref=got_in.at[k], send_sem=in_send.at[k],
            recv_sem=in_recv.at[k, 0], device_id={"mpo": z_in}, device_id_type=MESH,
        )
        in_copy_all.wait_send()

        @pl.when(jnp.logical_not(outer))
        def _():
            pltpu.make_async_remote_copy(
                src_ref=total.at[k], dst_ref=got_out.at[k], send_sem=out_send.at[k],
                recv_sem=out_recv.at[k, 0], device_id={"mpo": z_out}, device_id_type=MESH,
            ).wait_send()

    for k in range(STEPS):
        for d in range(1, n_peer):
            gram_copy(k, d, True).wait_send()

    def done_last(d, carry):
        last_copy(d, True).wait_send()
        return carry

    lax.fori_loop(1, n_all, done_last, 0)

    env_copy.wait()
    kept = env_own[pl.ds(pl.multiple_of(rep * share, share), share)] + env_recv[...].astype(F32)
    for w in range(terms):
        env_ref[w, 0] = kept[:, w * cols : (w + 1) * cols]


def local(n_mpo, n_sec, start_vector, block_rows, left_blocks, right_blocks):
    _, rows, cols = start_vector.shape
    terms, _, _, size = left_blocks.shape
    chunk = rows // CHUNKS
    n_peer = n_sec * 2
    n_all = n_mpo * n_peer
    dma = pltpu.SemaphoreType.DMA
    passing = pltpu.VMEM((ITERS, CHUNKS, chunk, cols), BF16)
    return pl.pallas_call(
        functools.partial(body, n_mpo, n_sec),
        out_shape=(
            jax.ShapeDtypeStruct((1, rows, cols), F32),
            jax.ShapeDtypeStruct((1,), F32),
            jax.ShapeDtypeStruct((terms, 1, cols // 2, cols), F32),
        ),
        in_specs=[
            pl.BlockSpec(memory_space=pltpu.SMEM),
            pl.BlockSpec(memory_space=pl.ANY),
            pl.BlockSpec(memory_space=pl.ANY),
            pl.BlockSpec(memory_space=pl.ANY),
        ],
        out_specs=(
            pl.BlockSpec(memory_space=pltpu.VMEM),
            pl.BlockSpec(memory_space=pltpu.SMEM),
            pl.BlockSpec(memory_space=pltpu.VMEM),
        ),
        scratch_shapes=[
            pltpu.VMEM((rows, cols), F32),
            pltpu.VMEM((terms, rows, size), BF16),
            pltpu.VMEM((terms, cols, cols), BF16),
            pltpu.VMEM((STEPS, rows, cols), F32),
            pltpu.VMEM((STEPS, size, cols), BF16),
            pltpu.VMEM((STEPS, rows, terms * cols), BF16),
            pltpu.VMEM((CHUNKS, chunk, cols), F32),
            pltpu.VMEM((8, 128), F32),
            passing,
            passing,
            passing,
            passing,
            pltpu.VMEM((STEPS, 8, cols), F32),
            pltpu.VMEM((STEPS, n_peer, 8, cols), F32),
            pltpu.VMEM((n_all, 8, 128), F32),
            pltpu.VMEM((cols, terms * cols), F32),
            pltpu.VMEM((cols // 2, terms * cols), BF16),
            pltpu.VMEM((cols // 2, terms * cols), BF16),
            dma((3,)),
            dma((STEPS,)),
            dma((STEPS,)),
            dma((ITERS,)),
            dma((ITERS, CHUNKS)),
            dma((ITERS,)),
            dma((ITERS, CHUNKS)),
            dma((STEPS,)),
            dma((STEPS, n_peer)),
            dma,
            dma((n_all,)),
            dma,
            dma,
        ],
        compiler_params=pltpu.CompilerParams(
            collective_id=0, has_side_effects=True, vmem_limit_bytes=50 * 2**20
        ),
    )(block_rows, start_vector, left_blocks, right_blocks)


def solution(mesh):
    return jax.shard_map(
        functools.partial(local, mesh.shape["mpo"], mesh.shape["sec"]),
        mesh=mesh,
        in_specs=(
            P(("groups", "sec"), "rep", None),
            P(("groups", "sec")),
            P("mpo", ("groups", "sec"), "rep", None),
            P("mpo", ("groups", "sec"), None, None),
        ),
        out_specs=(
            P(("groups", "sec"), "rep", None),
            P("groups"),
            P("mpo", ("groups", "sec"), "rep", None),
        ),
        check_vma=False,
    )
```

```python
import functools
import math

import jax
import jax.numpy as jnp
from jax import lax
from jax.experimental import pallas as pl
from jax.experimental.pallas import tpu as pltpu
from jax.sharding import PartitionSpec as P

ITERS = 4
EPSILON = 1e-06
STEPS = ITERS + 1
CHUNKS = 16
BLOCKS = 4
LAG = 8

F32 = jnp.float32
BF16 = jnp.bfloat16
MESH = pl.DeviceIdType.MESH


def body(
    n_mpo, n_sec, block_rows, start_hbm, left_hbm, right_hbm,
    wave_ref, energy_ref, env_ref,
    start_v, left, right, u, x, prod, term, inward, sums, total, got_in, got_out,
    acc, gram, last, env_own, env_send, env_recv,
    load_sem, x_send, x_recv, in_send, in_recv, out_send, out_recv,
    gram_send, gram_recv, last_send, last_recv, env_send_sem, env_recv_sem,
):
    terms, rows, size = left.shape
    cols = right.shape[1]
    chunk = rows // CHUNKS
    block = rows // BLOCKS
    per_block = CHUNKS // BLOCKS
    n_rep = 2
    n_peer = n_sec * n_rep
    n_all = n_mpo * n_peer
    half = n_mpo // 2

    z = lax.axis_index("mpo")
    sec = lax.axis_index("sec")
    rep = lax.axis_index("rep")
    peer = sec * n_rep + rep
    every = z * n_peer + peer
    other = 1 - rep
    lower = z < half
    depth = jnp.where(lower, z, n_mpo - 1 - z)
    z_in = jnp.where(lower, z + 1, z - 1)
    z_out = jnp.where(lower, z - 1, z + 1)
    middle = depth == half - 1
    outer = depth == 0
    own_at = pl.multiple_of(rep * rows, rows)
    other_at = pl.multiple_of(other * rows, rows)

    def device_at(index):
        return {
            "mpo": index // n_peer,
            "sec": lax.rem(index, n_peer) // n_rep,
            "rep": lax.rem(index, n_rep),
        }

    start_load = pltpu.make_async_copy(start_hbm.at[0], start_v, load_sem.at[0])
    left_load = pltpu.make_async_copy(left_hbm.at[:, 0], left, load_sem.at[1])
    right_load = pltpu.make_async_copy(right_hbm.at[:, 0], right, load_sem.at[2])
    start_load.start()
    left_load.start()
    right_load.start()

    barrier = pltpu.get_barrier_semaphore()

    def greet(d, carry):
        target = lax.rem(every + d, n_all)
        pl.semaphore_signal(barrier, inc=1, device_id=device_at(target), device_id_type=MESH)
        return carry

    lax.fori_loop(1, n_all, greet, 0)

    live_count = block_rows[0] - rep * rows
    row_at = lax.broadcasted_iota(jnp.int32, (chunk, cols), 0)

    def live_of(c):
        return row_at + c * chunk < live_count

    def x_copy(k, at, count):
        return pltpu.make_async_remote_copy(
            src_ref=x.at[k, pl.ds(at, count)],
            dst_ref=x.at[k, pl.ds(at, count)],
            send_sem=x_send.at[k],
            recv_sem=x_recv.at[k],
            device_id={"rep": other},
            device_id_type=MESH,
        )

    def in_copy(k, c, to_middle):
        if to_middle:
            return pltpu.make_async_remote_copy(
                src_ref=sums.at[k, c], dst_ref=got_out.at[k, c],
                send_sem=in_send.at[k], recv_sem=out_recv.at[k, c],
                device_id={"mpo": z_in}, device_id_type=MESH,
            )
        return pltpu.make_async_remote_copy(
            src_ref=sums.at[k, c], dst_ref=got_in.at[k, c],
            send_sem=in_send.at[k], recv_sem=in_recv.at[k, c],
            device_id={"mpo": z_in}, device_id_type=MESH,
        )

    def out_copy(k, c):
        return pltpu.make_async_remote_copy(
            src_ref=total.at[k, c], dst_ref=got_out.at[k, c],
            send_sem=out_send.at[k], recv_sem=out_recv.at[k, c],
            device_id={"mpo": z_out}, device_id_type=MESH,
        )

    def gram_copy(k, d, sending):
        target = lax.rem(peer + d, n_peer)
        slot = peer if sending else lax.rem(peer - d + n_peer, n_peer)
        return pltpu.make_async_remote_copy(
            src_ref=gram.at[k, slot], dst_ref=gram.at[k, slot],
            send_sem=gram_send.at[k], recv_sem=gram_recv.at[k, d],
            device_id={"sec": target // n_rep, "rep": lax.rem(target, n_rep)},
            device_id_type=MESH,
        )

    def last_copy(d, sending):
        target = lax.rem(every + d, n_all)
        slot = every if sending else lax.rem(every - d + n_all, n_all)
        return pltpu.make_async_remote_copy(
            src_ref=last.at[slot], dst_ref=last.at[slot],
            send_sem=last_send, recv_sem=last_recv.at[d],
            device_id=device_at(target), device_id_type=MESH,
        )

    def send_inward(k, c):
        if n_mpo == 2:
            in_copy(k, c, True).start()
            return

        @pl.when(middle)
        def _():
            in_copy(k, c, True).start()

        @pl.when(jnp.logical_not(middle))
        def _():
            in_copy(k, c, False).start()

    def fold(values):
        return jnp.sum(values.reshape(chunk // 8, 8, cols), axis=0)

    def put_basis(k, c, new):
        at = pl.multiple_of(c * chunk, chunk)
        u[k, pl.ds(at, chunk)] = new
        x_at = pl.multiple_of(own_at + c * chunk, chunk)
        x[k, pl.ds(x_at, chunk)] = new.astype(BF16)
        x_copy(k, x_at, chunk).start()
        for j in range(k):
            acc[j] += fold(new * u[j, pl.ds(at, chunk)])
        acc[k] += fold(new * new)

    def whole(values):
        one = jnp.sum(jnp.sum(values, axis=0, keepdims=True), axis=1, keepdims=True)
        return jnp.broadcast_to(one, (1, cols))

    def share_gram(k):
        parts = [whole(acc[j]) for j in range(k + 1)]
        parts += [jnp.zeros((8 - k - 1, cols), F32)]
        gram[k, peer] = jnp.concatenate(parts, axis=0)
        for d in range(1, n_peer):
            gram_copy(k, d, True).start()

    def take_gram(k):
        for d in range(1, n_peer):
            gram_copy(k, d, False).wait_recv()
        summed = gram[k, 0]
        for slot in range(1, n_peer):
            summed = summed + gram[k, slot]
        return [summed[j : j + 1] for j in range(k + 1)]

    def multiply(k):
        def one(b, carry):
            at = pl.multiple_of(b * block, block)
            for w in range(terms):
                left_term = jnp.dot(
                    left[w, pl.ds(at, block)], x[k], preferred_element_type=F32
                )
                prod[k, pl.ds(at, block), w * cols : (w + 1) * cols] = left_term.astype(BF16)
            group = jnp.dot(
                prod[k, pl.ds(at, block)],
                right[...].reshape(terms * cols, cols),
                preferred_element_type=F32,
            )
            if k < ITERS:
                for i in range(per_block):
                    piece = group[i * chunk : (i + 1) * chunk]
                    c = b * per_block + i

                    @pl.when(outer)
                    def _():
                        sums[k, c] = piece.astype(BF16)
                        send_inward(k, c)

                    @pl.when(jnp.logical_not(outer))
                    def _():
                        term[c] = piece
            else:
                held = group * u[k, pl.ds(at, block)]
                acc[0] += jnp.sum(held.reshape(block // 8, 8, cols), axis=0)
            return carry

        lax.fori_loop(0, BLOCKS, one, 0)

    ups, mids, downs, grams = [], [], [], {}

    def g(i, j):
        return grams[(min(i, j), max(i, j))]

    def coefficients(k):
        here = g(k, k) + EPSILON
        inverse = lax.rsqrt(here)
        if k == 0:
            mid = jnp.zeros_like(here)
            down = jnp.zeros_like(here)
        else:
            before = g(k - 1, k - 1) + EPSILON
            lean = ups[k - 1] * g(k - 1, k)
            if k >= 2:
                lean = lean + downs[k - 1] * g(k - 2, k - 1)
            mid = mids[k - 1] + lean / before
            down = ups[k - 1] * g(k, k) / before
        ups.append(here * inverse)
        mids.append(mid)
        downs.append(down)
        return inverse

    def combine(k, inverse):
        mid, down = mids[k], downs[k]

        def finish(c):
            @pl.when(middle)
            def _():
                out_copy(k, c).wait_recv()
                sides = sums[k, c].astype(F32) + got_out[k, c].astype(F32)
                total[k, c] = sides.astype(BF16)

            @pl.when(jnp.logical_not(middle))
            def _():
                out_copy(k, c).wait_recv()
                total[k, c] = got_out[k, c]

            @pl.when(jnp.logical_not(outer))
            def _():
                out_copy(k, c).start()

            at = pl.multiple_of(c * chunk, chunk)
            applied = jnp.where(live_of(c), total[k, c].astype(F32), 0.0)
            new = applied - mid * u[k, pl.ds(at, chunk)]
            if k >= 1:
                new = new - down * u[k - 1, pl.ds(at, chunk)]
            put_basis(k + 1, c, new * inverse)

        def one(c, carry):
            @pl.when(jnp.logical_and(jnp.logical_not(outer), c < CHUNKS))
            def _():
                in_copy(k, c, False).wait_recv()
                sums[k, c] = (term[c] + got_in[k, c].astype(F32)).astype(BF16)
                send_inward(k, c)

            @pl.when(c >= LAG)
            def _():
                finish(c - LAG)

            return carry

        lax.fori_loop(0, CHUNKS + LAG, one, 0)

    def dot_of(a, b):
        result = None
        for i, left_value in a.items():
            inner = None
            for j, right_value in b.items():
                value = right_value * g(i, j)
                inner = value if inner is None else inner + value
            value = left_value * inner
            result = value if result is None else result + value
        return result

    def applied_to(a):
        result = {}

        def add(i, value):
            result[i] = value if i not in result else result[i] + value

        for k, value in a.items():
            add(k + 1, ups[k] * value)
            if k >= 1:
                add(k, mids[k] * value)
                add(k - 1, downs[k] * value)
        return result

    def mixed(first, a, second, b):
        result = {i: first * value for i, value in a.items()}
        for i, value in b.items():
            scaled = second * value
            result[i] = scaled if i not in result else result[i] + scaled
        return result

    start_load.wait()
    pl.semaphore_wait(barrier, n_all - 1)
    acc[...] = jnp.zeros_like(acc)

    def begin(c, carry):
        at = pl.multiple_of(c * chunk, chunk)
        put_basis(0, c, jnp.where(live_of(c), start_v[pl.ds(at, chunk)], 0.0))
        return carry

    lax.fori_loop(0, CHUNKS, begin, 0)
    share_gram(0)
    left_load.wait()
    right_load.wait()

    state = {}
    for k in range(STEPS):
        x_copy(k, other_at, rows).wait_recv()
        if k == ITERS:
            acc[...] = jnp.zeros_like(acc)
        multiply(k)
        if k == ITERS:
            last[every] = jnp.broadcast_to(whole(acc[0])[:, :128], (8, 128))

            def send_last(d, carry):
                last_copy(d, True).start()
                return carry

            lax.fori_loop(1, n_all, send_last, 0)
        for j, value in enumerate(take_gram(k)):
            grams[(j, k)] = value
        if k < ITERS:
            inverse = coefficients(k)
        if k == 0:
            first = lax.rsqrt(g(0, 0) + EPSILON)
            state["vector"] = {0: first}
            state["applied"] = applied_to(state["vector"])
        if k == 1:
            state["rayleigh"] = dot_of(state["vector"], state["applied"])
        if k >= 1:
            vector, applied, rayleigh = state["vector"], state["applied"], state["rayleigh"]
            if k >= 2:
                residual, square_sum = state["residual"], state["square_sum"]
                scale, coupling = state["scale"], state["coupling"]
                image = applied_to(residual)
                product_sum = dot_of(residual, image)
                curvature = product_sum / (scale * scale)
                half_gap = 0.5 * (rayleigh - curvature)
                lowest = 0.5 * (rayleigh + curvature) - jnp.sqrt(half_gap * half_gap + coupling * coupling)
                retain = lowest - curvature
                length = jnp.sqrt(retain * retain + coupling * coupling)
                one, two = retain / length, coupling / (scale * length)
                vector = mixed(one, vector, two, residual)
                applied = mixed(one, applied, two, image)
                rayleigh = lowest
            residual = mixed(1.0, applied, -rayleigh, vector)
            square_sum = dot_of(residual, residual)
            scale = jnp.sqrt(square_sum + EPSILON)
            state = dict(
                vector=vector, applied=applied, rayleigh=rayleigh, residual=residual,
                square_sum=square_sum, scale=scale, coupling=square_sum / scale,
            )
        if k < ITERS:
            acc[...] = jnp.zeros_like(acc)
            combine(k, inverse)
            share_gram(k + 1)

    vector, rayleigh, residual = state["vector"], state["rayleigh"], state["residual"]
    scale, coupling = state["scale"], state["coupling"]
    top = residual[ITERS]
    lower_part = {i: value for i, value in residual.items() if i < ITERS}
    lower_image = applied_to(lower_part)
    known = dot_of(residual, lower_image) + top * dot_of({ITERS: jnp.ones_like(top)}, lower_image)
    inverse_square = 1.0 / (scale * scale)

    def take_last(d, carry):
        last_copy(d, False).wait_recv()
        return carry

    lax.fori_loop(1, n_all, take_last, 0)
    corner = lax.fori_loop(1, n_all, lambda i, value: value + last[i, 0:1], last[0, 0:1])
    corner = jnp.broadcast_to(corner[:, 0:1], (1, cols))
    curvature = (known + top * top * corner) * inverse_square
    half_gap = 0.5 * (rayleigh - curvature)
    lowest = 0.5 * (rayleigh + curvature) - jnp.sqrt(half_gap * half_gap + coupling * coupling)
    retain = lowest - curvature
    length = jnp.sqrt(retain * retain + coupling * coupling)
    full = math.sqrt(n_sec * size * cols)
    vector = mixed(full * retain / length, vector, full * coupling / (scale * length), residual)
    energy_ref[0] = lowest[0, 0]

    def finish_rows(c, carry):
        at = pl.multiple_of(c * chunk, chunk)
        here = pl.ds(at, chunk)
        wave = vector[0] * u[0, here]
        for k in range(1, STEPS):
            wave = wave + vector[k] * u[k, here]
        wave_ref[0, here] = wave
        x[0, here] = wave.astype(BF16)
        for w in range(terms):
            span = slice(w * cols, (w + 1) * cols)
            image = vector[0] * prod[0, here, span].astype(F32)
            for k in range(1, STEPS):
                image = image + vector[k] * prod[k, here, span].astype(F32)
            prod[0, here, span] = image.astype(BF16)
        return carry

    for k in range(STEPS):
        x_copy(k, own_at, rows).wait_send()
    lax.fori_loop(0, CHUNKS, finish_rows, 0)
    env_scale = math.sqrt(terms * n_mpo / size)
    env = lax.dot_general(
        x[0, 0:rows], prod[0], (((0,), (0,)), ((), ())), preferred_element_type=F32
    ) * env_scale
    env_own[...] = env
    share = cols // n_rep
    env_send[...] = env_own[pl.ds(pl.multiple_of(other * share, share), share)].astype(BF16)
    env_copy = pltpu.make_async_remote_copy(
        src_ref=env_send, dst_ref=env_recv, send_sem=env_send_sem, recv_sem=env_recv_sem,
        device_id={"rep": other}, device_id_type=MESH,
    )
    env_copy.start()

    for k in range(ITERS):
        in_copy_all = pltpu.make_async_remote_copy(
            src_ref=sums.at[k], dst_ref=got_in.at[k], send_sem=in_send.at[k],
            recv_sem=in_recv.at[k, 0], device_id={"mpo": z_in}, device_id_type=MESH,
        )
        in_copy_all.wait_send()

        @pl.when(jnp.logical_not(outer))
        def _():
            pltpu.make_async_remote_copy(
                src_ref=total.at[k], dst_ref=got_out.at[k], send_sem=out_send.at[k],
                recv_sem=out_recv.at[k, 0], device_id={"mpo": z_out}, device_id_type=MESH,
            ).wait_send()

    for k in range(STEPS):
        for d in range(1, n_peer):
            gram_copy(k, d, True).wait_send()

    def done_last(d, carry):
        last_copy(d, True).wait_send()
        return carry

    lax.fori_loop(1, n_all, done_last, 0)

    env_copy.wait()
    kept = env_own[pl.ds(pl.multiple_of(rep * share, share), share)] + env_recv[...].astype(F32)
    for w in range(terms):
        env_ref[w, 0] = kept[:, w * cols : (w + 1) * cols]


def local(n_mpo, n_sec, start_vector, block_rows, left_blocks, right_blocks):
    _, rows, cols = start_vector.shape
    terms, _, _, size = left_blocks.shape
    chunk = rows // CHUNKS
    n_peer = n_sec * 2
    n_all = n_mpo * n_peer
    dma = pltpu.SemaphoreType.DMA
    passing = pltpu.VMEM((ITERS, CHUNKS, chunk, cols), BF16)
    return pl.pallas_call(
        functools.partial(body, n_mpo, n_sec),
        out_shape=(
            jax.ShapeDtypeStruct((1, rows, cols), F32),
            jax.ShapeDtypeStruct((1,), F32),
            jax.ShapeDtypeStruct((terms, 1, cols // 2, cols), F32),
        ),
        in_specs=[
            pl.BlockSpec(memory_space=pltpu.SMEM),
            pl.BlockSpec(memory_space=pltpu.HBM),
            pl.BlockSpec(memory_space=pltpu.HBM),
            pl.BlockSpec(memory_space=pltpu.HBM),
        ],
        out_specs=(
            pl.BlockSpec(memory_space=pltpu.VMEM),
            pl.BlockSpec(memory_space=pltpu.SMEM),
            pl.BlockSpec(memory_space=pltpu.VMEM),
        ),
        scratch_shapes=[
            pltpu.VMEM((rows, cols), F32),
            pltpu.VMEM((terms, rows, size), BF16),
            pltpu.VMEM((terms, cols, cols), BF16),
            pltpu.VMEM((STEPS, rows, cols), F32),
            pltpu.VMEM((STEPS, size, cols), BF16),
            pltpu.VMEM((STEPS, rows, terms * cols), BF16),
            pltpu.VMEM((CHUNKS, chunk, cols), F32),
            pltpu.VMEM((8, 128), F32),
            passing,
            passing,
            passing,
            passing,
            pltpu.VMEM((STEPS, 8, cols), F32),
            pltpu.VMEM((STEPS, n_peer, 8, cols), F32),
            pltpu.VMEM((n_all, 8, 128), F32),
            pltpu.VMEM((cols, terms * cols), F32),
            pltpu.VMEM((cols // 2, terms * cols), BF16),
            pltpu.VMEM((cols // 2, terms * cols), BF16),
            dma((3,)),
            dma((STEPS,)),
            dma((STEPS,)),
            dma((ITERS,)),
            dma((ITERS, CHUNKS)),
            dma((ITERS,)),
            dma((ITERS, CHUNKS)),
            dma((STEPS,)),
            dma((STEPS, n_peer)),
            dma,
            dma((n_all,)),
            dma,
            dma,
        ],
        compiler_params=pltpu.CompilerParams(
            collective_id=0, has_side_effects=True, vmem_limit_bytes=62 * 2**20
        ),
    )(block_rows, start_vector, left_blocks, right_blocks)


def solution(mesh):
    return jax.shard_map(
        functools.partial(local, mesh.shape["mpo"], mesh.shape["sec"]),
        mesh=mesh,
        in_specs=(
            P(("groups", "sec"), "rep", None),
            P(("groups", "sec")),
            P("mpo", ("groups", "sec"), "rep", None),
            P("mpo", ("groups", "sec"), None, None),
        ),
        out_specs=(
            P(("groups", "sec"), "rep", None),
            P("groups"),
            P("mpo", ("groups", "sec"), "rep", None),
        ),
        check_vma=False,
    )
```

```python
import functools
import math

import jax
import jax.numpy as jnp
from jax import lax
from jax.experimental import pallas as pl
from jax.experimental.pallas import tpu as pltpu
from jax.sharding import PartitionSpec as P

ITERS = 4
EPSILON = 1e-06
STEPS = ITERS + 1
CHUNKS = 16
BLOCKS = 4
LAG = 7

F32 = jnp.float32
BF16 = jnp.bfloat16
MESH = pl.DeviceIdType.MESH


def body(
    n_mpo, n_sec, block_rows, start_hbm, left_hbm, right_hbm,
    wave_ref, energy_ref, env_ref,
    start_v, left, right, u, x, prod, term, inward, sums, total, got_in, got_out,
    acc, gram, last, env_own, env_send, env_recv,
    load_sem, x_send, x_recv, in_send, in_recv, out_send, out_recv,
    gram_send, gram_recv, last_send, last_recv, env_send_sem, env_recv_sem,
):
    terms, rows, size = left.shape
    cols = right.shape[1]
    chunk = rows // CHUNKS
    block = rows // BLOCKS
    per_block = CHUNKS // BLOCKS
    n_rep = 2
    n_peer = n_sec * n_rep
    n_all = n_mpo * n_peer
    half = n_mpo // 2

    z = lax.axis_index("mpo")
    sec = lax.axis_index("sec")
    rep = lax.axis_index("rep")
    peer = sec * n_rep + rep
    every = z * n_peer + peer
    other = 1 - rep
    lower = z < half
    depth = jnp.where(lower, z, n_mpo - 1 - z)
    z_in = jnp.where(lower, z + 1, z - 1)
    z_out = jnp.where(lower, z - 1, z + 1)
    middle = depth == half - 1
    outer = depth == 0
    own_at = pl.multiple_of(rep * rows, rows)
    other_at = pl.multiple_of(other * rows, rows)

    def device_at(index):
        return {
            "mpo": index // n_peer,
            "sec": lax.rem(index, n_peer) // n_rep,
            "rep": lax.rem(index, n_rep),
        }

    start_load = pltpu.make_async_copy(start_hbm.at[0], start_v, load_sem.at[0])
    left_load = pltpu.make_async_copy(left_hbm.at[:, 0], left, load_sem.at[1])
    right_load = pltpu.make_async_copy(right_hbm.at[:, 0], right, load_sem.at[2])
    start_load.start()
    left_load.start()
    right_load.start()

    barrier = pltpu.get_barrier_semaphore()

    def greet(d, carry):
        target = lax.rem(every + d, n_all)
        pl.semaphore_signal(barrier, inc=1, device_id=device_at(target), device_id_type=MESH)
        return carry

    lax.fori_loop(1, n_all, greet, 0)

    live_count = block_rows[0] - rep * rows
    row_at = lax.broadcasted_iota(jnp.int32, (chunk, cols), 0)

    def live_of(c):
        return row_at + c * chunk < live_count

    def x_copy(k, at, count):
        return pltpu.make_async_remote_copy(
            src_ref=x.at[k, pl.ds(at, count)],
            dst_ref=x.at[k, pl.ds(at, count)],
            send_sem=x_send.at[k],
            recv_sem=x_recv.at[k],
            device_id={"rep": other},
            device_id_type=MESH,
        )

    def in_copy(k, c, to_middle):
        if to_middle:
            return pltpu.make_async_remote_copy(
                src_ref=sums.at[k, c], dst_ref=got_out.at[k, c],
                send_sem=in_send.at[k], recv_sem=out_recv.at[k, c],
                device_id={"mpo": z_in}, device_id_type=MESH,
            )
        return pltpu.make_async_remote_copy(
            src_ref=sums.at[k, c], dst_ref=got_in.at[k, c],
            send_sem=in_send.at[k], recv_sem=in_recv.at[k, c],
            device_id={"mpo": z_in}, device_id_type=MESH,
        )

    def out_copy(k, c):
        return pltpu.make_async_remote_copy(
            src_ref=total.at[k, c], dst_ref=got_out.at[k, c],
            send_sem=out_send.at[k], recv_sem=out_recv.at[k, c],
            device_id={"mpo": z_out}, device_id_type=MESH,
        )

    def gram_copy(k, d, sending):
        target = lax.rem(peer + d, n_peer)
        slot = peer if sending else lax.rem(peer - d + n_peer, n_peer)
        return pltpu.make_async_remote_copy(
            src_ref=gram.at[k, slot], dst_ref=gram.at[k, slot],
            send_sem=gram_send.at[k], recv_sem=gram_recv.at[k, d],
            device_id={"sec": target // n_rep, "rep": lax.rem(target, n_rep)},
            device_id_type=MESH,
        )

    def last_copy(d, sending):
        target = lax.rem(every + d, n_all)
        slot = every if sending else lax.rem(every - d + n_all, n_all)
        return pltpu.make_async_remote_copy(
            src_ref=last.at[slot], dst_ref=last.at[slot],
            send_sem=last_send, recv_sem=last_recv.at[d],
            device_id=device_at(target), device_id_type=MESH,
        )

    def send_inward(k, c):
        if n_mpo == 2:
            in_copy(k, c, True).start()
            return

        @pl.when(middle)
        def _():
            in_copy(k, c, True).start()

        @pl.when(jnp.logical_not(middle))
        def _():
            in_copy(k, c, False).start()

    def fold(values):
        return jnp.sum(values.reshape(chunk // 8, 8, cols), axis=0)

    def put_basis(k, c, new):
        at = pl.multiple_of(c * chunk, chunk)
        u[k, pl.ds(at, chunk)] = new
        x_at = pl.multiple_of(own_at + c * chunk, chunk)
        x[k, pl.ds(x_at, chunk)] = new.astype(BF16)
        x_copy(k, x_at, chunk).start()
        for j in range(k):
            acc[j] += fold(new * u[j, pl.ds(at, chunk)])
        acc[k] += fold(new * new)

    def whole(values):
        one = jnp.sum(jnp.sum(values, axis=0, keepdims=True), axis=1, keepdims=True)
        return jnp.broadcast_to(one, (1, cols))

    def share_gram(k):
        parts = [whole(acc[j]) for j in range(k + 1)]
        parts += [jnp.zeros((8 - k - 1, cols), F32)]
        gram[k, peer] = jnp.concatenate(parts, axis=0)
        for d in range(1, n_peer):
            gram_copy(k, d, True).start()

    def take_gram(k):
        for d in range(1, n_peer):
            gram_copy(k, d, False).wait_recv()
        summed = gram[k, 0]
        for slot in range(1, n_peer):
            summed = summed + gram[k, slot]
        return [summed[j : j + 1] for j in range(k + 1)]

    def multiply(k):
        def one(b, carry):
            at = pl.multiple_of(b * block, block)
            for w in range(terms):
                left_term = jnp.dot(
                    left[w, pl.ds(at, block)], x[k], preferred_element_type=F32
                )
                prod[k, pl.ds(at, block), w * cols : (w + 1) * cols] = left_term.astype(BF16)
            group = jnp.dot(
                prod[k, pl.ds(at, block)],
                right[...].reshape(terms * cols, cols),
                preferred_element_type=F32,
            )
            if k < ITERS:
                for i in range(per_block):
                    piece = group[i * chunk : (i + 1) * chunk]
                    c = b * per_block + i

                    @pl.when(outer)
                    def _():
                        sums[k, c] = piece.astype(BF16)
                        send_inward(k, c)

                    @pl.when(jnp.logical_not(outer))
                    def _():
                        term[c] = piece
            else:
                held = group * u[k, pl.ds(at, block)]
                acc[0] += jnp.sum(held.reshape(block // 8, 8, cols), axis=0)
            return carry

        lax.fori_loop(0, BLOCKS, one, 0)

    ups, mids, downs, grams = [], [], [], {}

    def g(i, j):
        return grams[(min(i, j), max(i, j))]

    def coefficients(k):
        here = g(k, k) + EPSILON
        inverse = lax.rsqrt(here)
        if k == 0:
            mid = jnp.zeros_like(here)
            down = jnp.zeros_like(here)
        else:
            before = g(k - 1, k - 1) + EPSILON
            lean = ups[k - 1] * g(k - 1, k)
            if k >= 2:
                lean = lean + downs[k - 1] * g(k - 2, k - 1)
            mid = mids[k - 1] + lean / before
            down = ups[k - 1] * g(k, k) / before
        ups.append(here * inverse)
        mids.append(mid)
        downs.append(down)
        return inverse

    def combine(k, inverse):
        mid, down = mids[k], downs[k]

        def finish(c):
            @pl.when(middle)
            def _():
                out_copy(k, c).wait_recv()
                sides = sums[k, c].astype(F32) + got_out[k, c].astype(F32)
                total[k, c] = sides.astype(BF16)

            @pl.when(jnp.logical_not(middle))
            def _():
                out_copy(k, c).wait_recv()
                total[k, c] = got_out[k, c]

            @pl.when(jnp.logical_not(outer))
            def _():
                out_copy(k, c).start()

            at = pl.multiple_of(c * chunk, chunk)
            applied = jnp.where(live_of(c), total[k, c].astype(F32), 0.0)
            new = applied - mid * u[k, pl.ds(at, chunk)]
            if k >= 1:
                new = new - down * u[k - 1, pl.ds(at, chunk)]
            put_basis(k + 1, c, new * inverse)

        def one(c, carry):
            @pl.when(jnp.logical_and(jnp.logical_not(outer), c < CHUNKS))
            def _():
                in_copy(k, c, False).wait_recv()
                sums[k, c] = (term[c] + got_in[k, c].astype(F32)).astype(BF16)
                send_inward(k, c)

            @pl.when(c >= LAG)
            def _():
                finish(c - LAG)

            return carry

        lax.fori_loop(0, CHUNKS + LAG, one, 0)

    def dot_of(a, b):
        result = None
        for i, left_value in a.items():
            inner = None
            for j, right_value in b.items():
                value = right_value * g(i, j)
                inner = value if inner is None else inner + value
            value = left_value * inner
            result = value if result is None else result + value
        return result

    def applied_to(a):
        result = {}

        def add(i, value):
            result[i] = value if i not in result else result[i] + value

        for k, value in a.items():
            add(k + 1, ups[k] * value)
            if k >= 1:
                add(k, mids[k] * value)
                add(k - 1, downs[k] * value)
        return result

    def mixed(first, a, second, b):
        result = {i: first * value for i, value in a.items()}
        for i, value in b.items():
            scaled = second * value
            result[i] = scaled if i not in result else result[i] + scaled
        return result

    def advance(k, state):
        if k == 0:
            first = lax.rsqrt(g(0, 0) + EPSILON)
            state["vector"] = {0: first}
            state["applied"] = applied_to(state["vector"])
        if k == 1:
            state["rayleigh"] = dot_of(state["vector"], state["applied"])
        if k >= 1:
            vector, applied, rayleigh = state["vector"], state["applied"], state["rayleigh"]
            if k >= 2:
                residual, square_sum = state["residual"], state["square_sum"]
                scale, coupling = state["scale"], state["coupling"]
                image = applied_to(residual)
                product_sum = dot_of(residual, image)
                curvature = product_sum / (scale * scale)
                half_gap = 0.5 * (rayleigh - curvature)
                lowest = 0.5 * (rayleigh + curvature) - jnp.sqrt(half_gap * half_gap + coupling * coupling)
                retain = lowest - curvature
                length = jnp.sqrt(retain * retain + coupling * coupling)
                one, two = retain / length, coupling / (scale * length)
                vector = mixed(one, vector, two, residual)
                applied = mixed(one, applied, two, image)
                rayleigh = lowest
            residual = mixed(1.0, applied, -rayleigh, vector)
            square_sum = dot_of(residual, residual)
            scale = jnp.sqrt(square_sum + EPSILON)
            state = dict(
                vector=vector, applied=applied, rayleigh=rayleigh, residual=residual,
                square_sum=square_sum, scale=scale, coupling=square_sum / scale,
            )
        return state

    start_load.wait()
    pl.semaphore_wait(barrier, n_all - 1)
    acc[...] = jnp.zeros_like(acc)

    def begin(c, carry):
        at = pl.multiple_of(c * chunk, chunk)
        put_basis(0, c, jnp.where(live_of(c), start_v[pl.ds(at, chunk)], 0.0))
        return carry

    lax.fori_loop(0, CHUNKS, begin, 0)
    share_gram(0)
    left_load.wait()
    right_load.wait()

    state = {}
    for k in range(STEPS):
        x_copy(k, other_at, rows).wait_recv()
        if k == ITERS:
            acc[...] = jnp.zeros_like(acc)
        multiply(k)
        if k == ITERS:
            last[every] = jnp.broadcast_to(whole(acc[0])[:, :128], (8, 128))

            def send_last(d, carry):
                last_copy(d, True).start()
                return carry

            lax.fori_loop(1, n_all, send_last, 0)
        if k >= 1:
            state = advance(k - 1, state)
        for j, value in enumerate(take_gram(k)):
            grams[(j, k)] = value
        if k < ITERS:
            inverse = coefficients(k)
        if k < ITERS:
            acc[...] = jnp.zeros_like(acc)
            combine(k, inverse)
            share_gram(k + 1)

    state = advance(ITERS, state)

    vector, rayleigh, residual = state["vector"], state["rayleigh"], state["residual"]
    scale, coupling = state["scale"], state["coupling"]
    top = residual[ITERS]
    lower_part = {i: value for i, value in residual.items() if i < ITERS}
    lower_image = applied_to(lower_part)
    known = dot_of(residual, lower_image) + top * dot_of({ITERS: jnp.ones_like(top)}, lower_image)
    inverse_square = 1.0 / (scale * scale)

    def take_last(d, carry):
        last_copy(d, False).wait_recv()
        return carry

    lax.fori_loop(1, n_all, take_last, 0)
    corner = lax.fori_loop(1, n_all, lambda i, value: value + last[i, 0:1], last[0, 0:1])
    corner = jnp.broadcast_to(corner[:, 0:1], (1, cols))
    curvature = (known + top * top * corner) * inverse_square
    half_gap = 0.5 * (rayleigh - curvature)
    lowest = 0.5 * (rayleigh + curvature) - jnp.sqrt(half_gap * half_gap + coupling * coupling)
    retain = lowest - curvature
    length = jnp.sqrt(retain * retain + coupling * coupling)
    full = math.sqrt(n_sec * size * cols)
    vector = mixed(full * retain / length, vector, full * coupling / (scale * length), residual)
    energy_ref[0] = lowest[0, 0]

    def finish_rows(c, carry):
        at = pl.multiple_of(c * chunk, chunk)
        here = pl.ds(at, chunk)
        wave = vector[0] * u[0, here]
        for k in range(1, STEPS):
            wave = wave + vector[k] * u[k, here]
        wave_ref[0, here] = wave
        x[0, here] = wave.astype(BF16)
        for w in range(terms):
            span = slice(w * cols, (w + 1) * cols)
            image = vector[0] * prod[0, here, span].astype(F32)
            for k in range(1, STEPS):
                image = image + vector[k] * prod[k, here, span].astype(F32)
            prod[0, here, span] = image.astype(BF16)
        return carry

    for k in range(STEPS):
        x_copy(k, own_at, rows).wait_send()
    lax.fori_loop(0, CHUNKS, finish_rows, 0)
    env_scale = math.sqrt(terms * n_mpo / size)
    env = lax.dot_general(
        x[0, 0:rows], prod[0], (((0,), (0,)), ((), ())), preferred_element_type=F32
    ) * env_scale
    env_own[...] = env
    share = cols // n_rep
    env_send[...] = env_own[pl.ds(pl.multiple_of(other * share, share), share)].astype(BF16)
    env_copy = pltpu.make_async_remote_copy(
        src_ref=env_send, dst_ref=env_recv, send_sem=env_send_sem, recv_sem=env_recv_sem,
        device_id={"rep": other}, device_id_type=MESH,
    )
    env_copy.start()

    for k in range(ITERS):
        in_copy_all = pltpu.make_async_remote_copy(
            src_ref=sums.at[k], dst_ref=got_in.at[k], send_sem=in_send.at[k],
            recv_sem=in_recv.at[k, 0], device_id={"mpo": z_in}, device_id_type=MESH,
        )
        in_copy_all.wait_send()

        @pl.when(jnp.logical_not(outer))
        def _():
            pltpu.make_async_remote_copy(
                src_ref=total.at[k], dst_ref=got_out.at[k], send_sem=out_send.at[k],
                recv_sem=out_recv.at[k, 0], device_id={"mpo": z_out}, device_id_type=MESH,
            ).wait_send()

    for k in range(STEPS):
        for d in range(1, n_peer):
            gram_copy(k, d, True).wait_send()

    def done_last(d, carry):
        last_copy(d, True).wait_send()
        return carry

    lax.fori_loop(1, n_all, done_last, 0)

    env_copy.wait()
    kept = env_own[pl.ds(pl.multiple_of(rep * share, share), share)] + env_recv[...].astype(F32)
    for w in range(terms):
        env_ref[w, 0] = kept[:, w * cols : (w + 1) * cols]


def local(n_mpo, n_sec, start_vector, block_rows, left_blocks, right_blocks):
    _, rows, cols = start_vector.shape
    terms, _, _, size = left_blocks.shape
    chunk = rows // CHUNKS
    n_peer = n_sec * 2
    n_all = n_mpo * n_peer
    dma = pltpu.SemaphoreType.DMA
    passing = pltpu.VMEM((ITERS, CHUNKS, chunk, cols), BF16)
    return pl.pallas_call(
        functools.partial(body, n_mpo, n_sec),
        out_shape=(
            jax.ShapeDtypeStruct((1, rows, cols), F32),
            jax.ShapeDtypeStruct((1,), F32),
            jax.ShapeDtypeStruct((terms, 1, cols // 2, cols), F32),
        ),
        in_specs=[
            pl.BlockSpec(memory_space=pltpu.SMEM),
            pl.BlockSpec(memory_space=pltpu.HBM),
            pl.BlockSpec(memory_space=pltpu.HBM),
            pl.BlockSpec(memory_space=pltpu.HBM),
        ],
        out_specs=(
            pl.BlockSpec(memory_space=pltpu.VMEM),
            pl.BlockSpec(memory_space=pltpu.SMEM),
            pl.BlockSpec(memory_space=pltpu.VMEM),
        ),
        scratch_shapes=[
            pltpu.VMEM((rows, cols), F32),
            pltpu.VMEM((terms, rows, size), BF16),
            pltpu.VMEM((terms, cols, cols), BF16),
            pltpu.VMEM((STEPS, rows, cols), F32),
            pltpu.VMEM((STEPS, size, cols), BF16),
            pltpu.VMEM((STEPS, rows, terms * cols), BF16),
            pltpu.VMEM((CHUNKS, chunk, cols), F32),
            pltpu.VMEM((8, 128), F32),
            passing,
            passing,
            passing,
            passing,
            pltpu.VMEM((STEPS, 8, cols), F32),
            pltpu.VMEM((STEPS, n_peer, 8, cols), F32),
            pltpu.VMEM((n_all, 8, 128), F32),
            pltpu.VMEM((cols, terms * cols), F32),
            pltpu.VMEM((cols // 2, terms * cols), BF16),
            pltpu.VMEM((cols // 2, terms * cols), BF16),
            dma((3,)),
            dma((STEPS,)),
            dma((STEPS,)),
            dma((ITERS,)),
            dma((ITERS, CHUNKS)),
            dma((ITERS,)),
            dma((ITERS, CHUNKS)),
            dma((STEPS,)),
            dma((STEPS, n_peer)),
            dma,
            dma((n_all,)),
            dma,
            dma,
        ],
        compiler_params=pltpu.CompilerParams(
            collective_id=0, has_side_effects=True, vmem_limit_bytes=62 * 2**20
        ),
    )(block_rows, start_vector, left_blocks, right_blocks)


def solution(mesh):
    return jax.shard_map(
        functools.partial(local, mesh.shape["mpo"], mesh.shape["sec"]),
        mesh=mesh,
        in_specs=(
            P(("groups", "sec"), "rep", None),
            P(("groups", "sec")),
            P("mpo", ("groups", "sec"), "rep", None),
            P("mpo", ("groups", "sec"), None, None),
        ),
        out_specs=(
            P(("groups", "sec"), "rep", None),
            P("groups"),
            P("mpo", ("groups", "sec"), "rep", None),
        ),
        check_vma=False,
    )
```
